32 devices in a mesh: wx: 8 (over y, x, core), ny: 4 (over z).
Axes of the slice: x: 2, y: 2, z: 4, core: 2. Of those that a mesh axis runs over, the one named last changes fastest.
Arguments:
- displacement: float32 [3, 32, 6, 512], P(None, 'wx', None, 'ny'), may hold values from -0.1 to 0.1
- velocity: float32 [3, 32, 6, 512], P(None, 'wx', None, 'ny'), may hold values from -1 to 1
- labels: int32 [32, 6, 512], P('wx', None, 'ny'), may hold values from 0 to 7
- bond_mask: int32 [61, 32, 6, 512], P(None, 'wx', None, 'ny'), may hold values 0 or 1
- stiffness: float32 [8], replicated, may hold values from 1 to 10
- critical: float32 [8], replicated, may hold values from 0.02 to 0.2
Outputs:
- final_displacement: float32 [3, 32, 6, 512], P(None, 'wx', None, 'ny')
- final_velocity: float32 [3, 32, 6, 512], P(None, 'wx', None, 'ny')
The draws below stay inside these ranges and needn't reach their ends.
All inputs are finite; a program needn't handle non-finite values. No bound on the sum of `bond_mask` on one device may be relied on, other than what follows from the above.
Results may differ from the reference program's by a relative error of at most 0.00002.
Values sent between devices are 32-bit elements; how exact they have to be, the bound alone decides.
A program may use at most 64 MiB of HBM per device.

```python
import math
import jax
import jax.numpy as jnp

NZ = 6
STEPS = 3
MATS = 8
OFFSETS = 61
NX = 32
NY = 512


def touch_ends(result, stream_key, smallest, top_value):
    shape = result.shape
    index_at = [jax.random.randint(jax.random.fold_in(stream_key, axis), (), 0, shape[axis]) for axis in range(len(shape))]
    result = result.at[tuple(index_at)].set(smallest)
    longest = shape.index(max(shape))
    index_at[longest] = (index_at[longest] + 1) % shape[longest]
    return result.at[tuple(index_at)].set(top_value)


def block_levels(rng, extent, shards, smallest, largest):
    gain, own = 1.0, jax.random.fold_in(rng, 6)
    for dim, shards_of in shards:
        steps = jnp.exp(jax.random.uniform(jax.random.fold_in(own, dim), (shards_of,), jnp.float32, smallest / len(shards), largest / len(shards)))
        gain = gain * jnp.repeat(steps, extent[dim] // shards_of).reshape([-1 if axis == dim else 1 for axis in range(len(extent))])
    return gain


def scatter_about(stream_key, extent, width, limit, cuts=(), kind=jnp.bfloat16):
    values = jax.random.normal(stream_key, extent, jnp.float32) * width
    if len(cuts) > 0:
        values = block_levels(stream_key, extent, cuts, -0.22, 0.18) * values
    return jnp.clip(values, min=-limit, max=limit).astype(kind)


def setup_inputs(seed: int = 0) -> dict:
    streams_of = jax.random.split(jax.random.key(seed), 7)
    return {
        "displacement": scatter_about(streams_of[0], (3, NX, NZ, NY), 0.02, 0.1, ((1, 8), (3, 4)), jnp.float32),
        "velocity": scatter_about(streams_of[1], (3, NX, NZ, NY), 0.2, 1.0, ((1, 8), (3, 4)), jnp.float32),
        "labels": touch_ends(jax.random.randint(streams_of[2], (NX, NZ, NY), 0, MATS), jax.random.fold_in(streams_of[2], 1), 0, MATS - 1).astype(jnp.int32),
        "bond_mask": touch_ends((jax.random.randint(streams_of[3], (OFFSETS, NX, NZ, NY), 0, 10) < 9).astype(jnp.int32), jax.random.fold_in(streams_of[3], 1), 0, 1),
        "stiffness": jnp.clip(jnp.exp(jax.random.uniform(streams_of[4], (MATS,), jnp.float32, math.log(1.0), math.log(10.0))), 1.0, 10.0),
        "critical": jnp.clip(jnp.exp(jax.random.uniform(streams_of[5], (MATS,), jnp.float32, math.log(0.02), math.log(0.2))), 0.02, 0.2),
    }


time_step = 0.05

def bond_offsets():
    chosen = []
    for step_x in range(0, 4):
        for step_z in range(-3, 4):
            for step_y in range(-3, 4):
                if step_x * step_x + step_z * step_z + step_y * step_y <= 9:
                    if step_x > 0 or (step_x == 0 and (step_z > 0 or (step_z == 0 and step_y > 0))):
                        chosen.append((step_x, step_z, step_y))
    return chosen

def node_material(labels, stiffness, critical):
    modulus = jnp.zeros(labels.shape, jnp.float32)
    strain_limit = jnp.zeros(labels.shape, jnp.float32)
    for material in range(MATS):
        matches = labels == material
        modulus = jnp.where(matches, stiffness[material], modulus)
        strain_limit = jnp.where(matches, critical[material], strain_limit)
    return (modulus, strain_limit)

def pair_force(offset, source, target, modulus_here, modulus_there, limit_here, limit_there, intact):
    length = math.sqrt(offset[0] * offset[0] + offset[1] * offset[1] + offset[2] * offset[2])
    relative = [float(offset[component]) + target[component] - source[component] for component in range(3)]
    distance = jnp.sqrt(relative[0] * relative[0] + relative[1] * relative[1] + relative[2] * relative[2])
    stretch = (distance - length) / length
    pair_modulus = 2.0 * modulus_here * modulus_there / (modulus_here + modulus_there)
    pair_limit = 0.5 * (limit_here + limit_there)
    ratio = stretch / pair_limit
    magnitude = intact * pair_modulus * stretch / (1.0 + ratio * ratio) / (length * length)
    return jnp.stack([magnitude * part for part in relative])

def total_force(displacement, modulus, strain_limit, bond_mask):
    padded = jnp.pad(displacement, ((0, 0), (3, 3), (3, 3), (3, 3)))
    modulus_pad = jnp.pad(modulus, 3)
    limit_pad = jnp.pad(strain_limit, 3)
    index_x = jnp.arange(NX, dtype=jnp.int32).reshape(NX, 1, 1)
    index_z = jnp.arange(NZ, dtype=jnp.int32).reshape(1, NZ, 1)
    index_y = jnp.arange(NY, dtype=jnp.int32).reshape(1, 1, NY)
    spread = jnp.zeros(padded.shape, jnp.float32)
    force_here = jnp.zeros(displacement.shape, jnp.float32)
    for number, offset in enumerate(bond_offsets()):
        step_x, step_z, step_y = offset
        low_x, low_z, low_y = (3 + step_x, 3 + step_z, 3 + step_y)
        target = padded[:, low_x:low_x + NX, low_z:low_z + NZ, low_y:low_y + NY]
        modulus_there = modulus_pad[low_x:low_x + NX, low_z:low_z + NZ, low_y:low_y + NY]
        limit_there = limit_pad[low_x:low_x + NX, low_z:low_z + NZ, low_y:low_y + NY]
        inside = (index_x + step_x >= 0) & (index_x + step_x < NX)
        inside = inside & (index_z + step_z >= 0) & (index_z + step_z < NZ)
        inside = inside & (index_y + step_y >= 0) & (index_y + step_y < NY)
        intact = jnp.where(inside, bond_mask[number], 0).astype(jnp.float32)
        force = pair_force(offset, displacement, target, modulus, modulus_there, strain_limit, limit_there, intact)
        force_here = force_here + force
        spread = spread.at[:, low_x:low_x + NX, low_z:low_z + NZ, low_y:low_y + NY].add(-force)
    return force_here + spread[:, 3:3 + NX, 3:3 + NZ, 3:3 + NY]

def reference(displacement, velocity, labels, bond_mask, stiffness, critical):
    modulus, strain_limit = node_material(labels, stiffness, critical)
    for repeat in range(STEPS):
        force = total_force(displacement, modulus, strain_limit, bond_mask)
        velocity = velocity + time_step * force
        displacement = displacement + time_step * velocity
    return (displacement, velocity)
```

```python
import functools
import math

import jax
import jax.numpy as jnp
from jax import lax
from jax.experimental import pallas as pl
from jax.experimental.pallas import tpu as pltpu
from jax.sharding import PartitionSpec as P

STEPS = 3
MATS = 8
time_step = 0.05
MESH = pl.DeviceIdType.MESH
DIRECTIONS = [(dx, dy) for dx in (-1, 0, 1) for dy in (-1, 0, 1) if (dx, dy) != (0, 0)]


def bond_offsets():
    chosen = []
    for step_x in range(0, 4):
        for step_z in range(-3, 4):
            for step_y in range(-3, 4):
                if step_x * step_x + step_z * step_z + step_y * step_y <= 9:
                    if step_x > 0 or (step_x == 0 and (step_z > 0 or (step_z == 0 and step_y > 0))):
                        chosen.append((step_x, step_z, step_y))
    return chosen


OFFSETS = bond_offsets()
SLOT = {}
for _sign in (1, -1):
    for _k in [k for k, d in enumerate(OFFSETS) if d[2] * _sign > 0]:
        SLOT[_k] = sum(1 for q in SLOT if OFFSETS[q][2] * _sign > 0)
SHELL = sorted(
    [(k, True, d) for k, d in enumerate(OFFSETS)]
    + [(k, False, (-d[0], -d[1], -d[2])) for k, d in enumerate(OFFSETS)],
    key=lambda item: item[2],
)
GROUPS = {
    a: [k for k, d in enumerate(OFFSETS) if d[0] == a] for a in sorted({d[0] for d in OFFSETS}) if a > 0
}


def kernel(
    shape,
    disp_in, vel_in, lab_in, mask_in, stiff, crit,
    disp_out, vel_out,
    ext, edge_send, edge_land, mat_ext, mat_send, mat_land,
    mask_x1, mask_x2, mask_x3, mask_ext, pack_send, pack_land,
    moved, mat_moved, gain, spread, vel,
    send_sem, recv_sem, mat_ssem, mat_rsem, mx_ssem, mx_rsem, pk_ssem, pk_rsem,
):
    nx, nz, ny = shape
    rows = nx * nz
    size_x, size_y = lax.axis_size("wx"), lax.axis_size("ny")
    my_x, my_y = lax.axis_index("wx"), lax.axis_index("ny")
    lane = lax.broadcasted_iota(jnp.int32, (rows, ny), 1)
    row = lax.broadcasted_iota(jnp.int32, (rows, ny), 0)
    depth = row % nz
    mask_x = (mask_x1, mask_x2, mask_x3)

    def roll(value, shift):
        shift = shift % ny
        return value if shift == 0 else pltpu.roll(value, shift, 1)

    def exists(dx, dy):
        ok = my_x >= 0
        if dx != 0:
            ok = (my_x + dx >= 0) & (my_x + dx < size_x)
        if dy != 0:
            ok = ok & (my_y + dy >= 0) & (my_y + dy < size_y)
        return ok

    ext[...] = jnp.zeros_like(ext)
    edge_land[...] = jnp.zeros_like(edge_land)
    mat_ext[...] = jnp.zeros_like(mat_ext)
    mat_land[...] = jnp.zeros_like(mat_land)
    pack_land[...] = jnp.zeros_like(pack_land)
    for ref in mask_x:
        ref[...] = jnp.zeros_like(ref)

    barrier = pltpu.get_barrier_semaphore()
    for dx, dy in DIRECTIONS:
        @pl.when(exists(dx, dy))
        def _(dx=dx, dy=dy):
            pl.semaphore_signal(
                barrier, inc=1, device_id=(my_x + dx, my_y + dy), device_id_type=MESH
            )

    def pack_edges(fields, target):
        up = jnp.zeros((rows, ny), jnp.float32)
        down = jnp.zeros((rows, ny), jnp.float32)
        for f, value in enumerate(fields):
            up = jnp.where(lane // 4 == ny // 4 - 1 - f, roll(value, -4 * f), up)
            down = jnp.where(lane // 4 == f, roll(value, 4 * f), down)
        target[0] = up
        target[1] = down

    def halo_copies(whole, sent, land, ssem, rsem):
        copies = []
        for index, (dx, dy) in enumerate(DIRECTIONS):
            place = pl.ds((1 - dx) * rows, rows)
            if dy == 0:
                source = whole.at[:, pl.ds(rows, rows), :]
                target = whole.at[:, place, :]
            else:
                side = 0 if dy > 0 else 1
                source = sent.at[side]
                target = land.at[side, place, :]
            copy = pltpu.make_async_remote_copy(
                src_ref=source, dst_ref=target, send_sem=ssem.at[index], recv_sem=rsem.at[index],
                device_id=(my_x + dx, my_y + dy), device_id_type=MESH,
            )
            copies.append((dx, dy, copy))
        return copies

    def mask_copies():
        copies = []
        for number, (a, members) in enumerate(GROUPS.items()):
            copies.append((1, 0, pltpu.make_async_remote_copy(
                src_ref=mask_in.at[pl.ds(members[0], len(members)), pl.ds(nx - a, a)],
                dst_ref=mask_x[number],
                send_sem=mx_ssem.at[number], recv_sem=mx_rsem.at[number],
                device_id=(my_x + 1, my_y), device_id_type=MESH,
            )))
        return copies

    def pack_copies():
        copies = []
        for index, (dx, dy) in enumerate([(0, 1), (0, -1), (1, 1), (1, -1)]):
            side = 0 if dy > 0 else 1
            copies.append((dx, dy, pltpu.make_async_remote_copy(
                src_ref=pack_send.at[side],
                dst_ref=pack_land.at[side, pl.ds((1 - dx) * rows, rows), :],
                send_sem=pk_ssem.at[index], recv_sem=pk_rsem.at[index],
                device_id=(my_x + dx, my_y + dy), device_id_type=MESH,
            )))
        return copies

    def start(copies):
        for dx, dy, copy in copies:
            pl.when(exists(dx, dy))(copy.start)

    def arrive(copies):
        for dx, dy, copy in copies:
            pl.when(exists(-dx, -dy))(copy.wait_recv)

    def leave(copies):
        for dx, dy, copy in copies:
            pl.when(exists(dx, dy))(copy.wait_send)

    def step_copies(s):
        return halo_copies(ext.at[s], edge_send.at[s], edge_land.at[s], send_sem.at[s], recv_sem.at[s])

    mat_copies = halo_copies(mat_ext, mat_send, mat_land, mat_ssem, mat_rsem)

    for x in range(nx):
        at = pl.ds(rows + x * nz, nz)
        for f in range(3):
            ext[0, f, at, :] = disp_in[f, x]
            vel[f, pl.ds(x * nz, nz), :] = vel_in[f, x]
        labels = lab_in[x]
        modulus = jnp.zeros(labels.shape, jnp.float32)
        limit = jnp.zeros(labels.shape, jnp.float32)
        for material in range(MATS):
            matches = labels == material
            modulus = jnp.where(matches, stiff[material], modulus)
            limit = jnp.where(matches, crit[material], limit)
        mat_ext[0, at, :] = modulus
        mat_ext[1, at, :] = limit
    own = pl.ds(rows, rows)
    pack_edges([mat_ext[f, own, :] for f in range(2)], mat_send)
    pack_edges([ext[0, f, own, :] for f in range(3)], edge_send.at[0])

    neighbours = lax.select(my_x > 0, 1, 0) + lax.select(my_x < size_x - 1, 1, 0) + 1
    neighbours = neighbours * (lax.select(my_y > 0, 1, 0) + lax.select(my_y < size_y - 1, 1, 0) + 1) - 1
    pl.semaphore_wait(barrier, neighbours)
    start(mat_copies)
    start(mask_copies())
    start(step_copies(0))

    up = jnp.zeros((rows, ny), jnp.float32)
    down = jnp.zeros((rows, ny), jnp.float32)
    for k, d in enumerate(OFFSETS):
        for x in range(nx):
            mask_ext[k, pl.ds(rows + x * nz, nz), :] = mask_in[k, x].astype(jnp.float32)
        c = d[2]
        if c > 0:
            value = mask_ext[k, own, :]
            up = jnp.where(lane // 4 == SLOT[k], roll(value, c + 4 * SLOT[k]), up)
        elif c < 0:
            value = mask_ext[k, own, :]
            down = jnp.where(lane // 4 == ny // 4 - 1 - SLOT[k], roll(value, c - 4 * SLOT[k]), down)
    pack_send[0] = up
    pack_send[1] = down
    start(pack_copies())

    def shift_fields(source, land, target, count, add_step):
        full = 3 * rows
        lanes = lax.broadcasted_iota(jnp.int32, (full, ny), 1)
        for f in range(count):
            value = source[f]
            high = roll(land[1], -4 * f)
            low = roll(land[0], 4 * f)
            for c in range(-3, 4):
                moved_value = value
                if c > 0:
                    moved_value = roll(jnp.where(lanes < c, high, value), -c)
                elif c < 0:
                    moved_value = roll(jnp.where(lanes >= ny + c, low, value), -c)
                if add_step and f == 2 and c != 0:
                    moved_value = moved_value + float(c)
                target[c + 3, f] = moved_value

    arrive(mat_copies)
    shift_fields(mat_ext, mat_land, mat_moved, 2, False)

    def inside_depth(b):
        return jnp.where((depth + b >= 0) & (depth + b < nz), 1.0, 0.0).astype(jnp.float32)

    def coefficients(number, offset, live):
        a, b, c = offset
        length = math.sqrt(a * a + b * b + c * c)
        at = pl.ds(rows + nz * a + b, rows)
        here, there = mat_ext[0, own, :], mat_moved[c + 3, 0, at, :]
        limit = mat_ext[1, own, :] + mat_moved[c + 3, 1, at, :]
        square = limit * limit * (0.25 * length * length)
        if b != 0:
            live = live * inside_depth(b)
        gain[number] = (here * there) / (here + there) * (square * (2.0 / length**3)) * live
        spread[number] = square

    for number, (k, forward, offset) in enumerate(SHELL):
        if forward:
            coefficients(number, offset, mask_ext[k, own, :])

    arrive(mask_copies())
    arrive(pack_copies())
    for number, (a, members) in enumerate(GROUPS.items()):
        for place, k in enumerate(members):
            mask_ext[k, pl.ds(0, rows), :] = jnp.zeros((rows, ny), jnp.float32)
            for x in range(a):
                mask_ext[k, pl.ds((nx - a + x) * nz, nz), :] = mask_x[number][place, x].astype(jnp.float32)
    for k in range(GROUPS[1][0]):
        mask_ext[k, pl.ds(0, rows), :] = jnp.zeros((rows, ny), jnp.float32)
    for number, (k, forward, offset) in enumerate(SHELL):
        if not forward:
            a, b, c = OFFSETS[k]
            at = pl.ds(rows - nz * a - b, rows)
            live = roll(mask_ext[k, at, :], c)
            if c > 0:
                live = jnp.where(lane < c, roll(pack_land[0, at, :], -4 * SLOT[k]), live)
            elif c < 0:
                live = jnp.where(lane >= ny + c, roll(pack_land[1, at, :], 4 * SLOT[k]), live)
            coefficients(number, offset, live)

    def one_step(s, carry):
        arrive(step_copies(s))
        shift_fields(ext.at[s], edge_land.at[s], moved, 3, True)
        here = [ext[s, f, own, :] for f in range(3)]
        force = [jnp.zeros((rows, ny), jnp.float32) for _ in range(3)]
        for number, (k, forward, offset) in enumerate(SHELL):
            a, b, c = offset
            length = math.sqrt(a * a + b * b + c * c)
            at = pl.ds(rows + nz * a + b, rows)
            e = [
                moved[c + 3, 0, at, :] - (here[0] - float(a)),
                moved[c + 3, 1, at, :] - (here[1] - float(b)),
                moved[c + 3, 2, at, :] - here[2],
            ]
            square = jnp.maximum(e[0] * e[0] + e[1] * e[1] + e[2] * e[2], 1e-30)
            t = square * lax.rsqrt(square) - length
            magnitude = gain[number] * t / (spread[number] + t * t)
            force = [force[f] + magnitude * e[f] for f in range(3)]
        fresh = []
        for f in range(3):
            velocity = vel[f] + time_step * force[f]
            vel[f] = velocity
            fresh.append(here[f] + time_step * velocity)

        @pl.when(s < STEPS - 1)
        def _():
            for f in range(3):
                ext[s + 1, f, own, :] = fresh[f]
            pack_edges(fresh, edge_send.at[s + 1])
            start(step_copies(s + 1))

        @pl.when(s == STEPS - 1)
        def _():
            for f in range(3):
                moved[3, f, pl.ds(0, rows), :] = fresh[f]
        return carry

    lax.fori_loop(0, STEPS, one_step, 0)
    for f in range(3):
        for x in range(nx):
            disp_out[f, x] = moved[3, f, pl.ds(x * nz, nz), :]
            vel_out[f, x] = vel[f, pl.ds(x * nz, nz), :]

    leave(mat_copies)
    leave(mask_copies())
    leave(pack_copies())

    def drain(s, carry):
        leave(step_copies(s))
        return carry

    lax.fori_loop(0, STEPS, drain, 0)


def on_device(displacement, velocity, labels, bond_mask, stiffness, critical):
    nx, nz, ny = labels.shape
    rows = nx * nz
    count = len(SHELL)
    f32 = jnp.float32
    vmem, smem = pl.BlockSpec(memory_space=pltpu.VMEM), pl.BlockSpec(memory_space=pltpu.SMEM)
    dma = pltpu.SemaphoreType.DMA
    return pl.pallas_call(
        functools.partial(kernel, (nx, nz, ny)),
        out_shape=[jax.ShapeDtypeStruct(displacement.shape, f32)] * 2,
        in_specs=[vmem] * 4 + [smem] * 2,
        out_specs=[vmem] * 2,
        scratch_shapes=[
            pltpu.VMEM((STEPS, 3, 3 * rows, ny), f32),
            pltpu.VMEM((STEPS, 2, rows, ny), f32),
            pltpu.VMEM((STEPS, 2, 3 * rows, ny), f32),
            pltpu.VMEM((2, 3 * rows, ny), f32),
            pltpu.VMEM((2, rows, ny), f32),
            pltpu.VMEM((2, 3 * rows, ny), f32),
            pltpu.VMEM((len(GROUPS[1]), 1, nz, ny), jnp.int32),
            pltpu.VMEM((len(GROUPS[2]), 2, nz, ny), jnp.int32),
            pltpu.VMEM((len(GROUPS[3]), 3, nz, ny), jnp.int32),
            pltpu.VMEM((len(OFFSETS), 2 * rows, ny), f32),
            pltpu.VMEM((2, rows, ny), f32),
            pltpu.VMEM((2, 2 * rows, ny), f32),
            pltpu.VMEM((7, 3, 3 * rows, ny), f32),
            pltpu.VMEM((7, 2, 3 * rows, ny), f32),
            pltpu.VMEM((count, rows, ny), f32),
            pltpu.VMEM((count, rows, ny), f32),
            pltpu.VMEM((3, rows, ny), f32),
            dma((STEPS, 8)), dma((STEPS, 8)), dma((8,)), dma((8,)),
            dma((3,)), dma((3,)), dma((4,)), dma((4,)),
        ],
        compiler_params=pltpu.CompilerParams(
            collective_id=0, has_side_effects=True, vmem_limit_bytes=40 * 1024 * 1024
        ),
        name="peridynamics",
    )(displacement, velocity, labels, bond_mask, stiffness, critical)


def solution(mesh):
    in_specs = (
        P(None, "wx", None, "ny"),
        P(None, "wx", None, "ny"),
        P("wx", None, "ny"),
        P(None, "wx", None, "ny"),
        P(),
        P(),
    )
    out_specs = (P(None, "wx", None, "ny"), P(None, "wx", None, "ny"))
    return jax.shard_map(
        on_device, mesh=mesh, in_specs=in_specs, out_specs=out_specs, check_vma=False
    )
```

```python
import functools
import math

import jax
import jax.numpy as jnp
from jax import lax
from jax.experimental import pallas as pl
from jax.experimental.pallas import tpu as pltpu
from jax.sharding import PartitionSpec as P

STEPS = 3
MATS = 8
time_step = 0.05
MESH = pl.DeviceIdType.MESH
DIRECTIONS = [(dx, dy) for dx in (-1, 0, 1) for dy in (-1, 0, 1) if (dx, dy) != (0, 0)]


def bond_offsets():
    chosen = []
    for step_x in range(0, 4):
        for step_z in range(-3, 4):
            for step_y in range(-3, 4):
                if step_x * step_x + step_z * step_z + step_y * step_y <= 9:
                    if step_x > 0 or (step_x == 0 and (step_z > 0 or (step_z == 0 and step_y > 0))):
                        chosen.append((step_x, step_z, step_y))
    return chosen


OFFSETS = bond_offsets()
SLOT = {}
for _sign in (1, -1):
    for _k in [k for k, d in enumerate(OFFSETS) if d[2] * _sign > 0]:
        SLOT[_k] = sum(1 for q in SLOT if OFFSETS[q][2] * _sign > 0)
SHELL = sorted(
    [(k, True, d) for k, d in enumerate(OFFSETS)]
    + [(k, False, (-d[0], -d[1], -d[2])) for k, d in enumerate(OFFSETS)],
    key=lambda item: item[2],
)
FLAT = sum(1 for d in OFFSETS if d[0] == 0)


def kernel(
    shape,
    disp_in, vel_in, lab_in, mask_in, stiff, crit,
    disp_out, vel_out,
    ext, edge_send, edge_land, mat_ext, mat_send, mat_land,
    mask_send, mask_land, mask_ext, pack_send, pack_land,
    moved, mat_moved, gain, spread, vel,
    send_sem, recv_sem, mat_ssem, mat_rsem, mx_ssem, mx_rsem, pk_ssem, pk_rsem,
):
    nx, nz, ny = shape
    rows = nx * nz
    size_x, size_y = lax.axis_size("wx"), lax.axis_size("ny")
    my_x, my_y = lax.axis_index("wx"), lax.axis_index("ny")
    lane = lax.broadcasted_iota(jnp.int32, (rows, ny), 1)
    row = lax.broadcasted_iota(jnp.int32, (rows, ny), 0)
    depth = row % nz

    def layer(x):
        return pl.ds(x, nz, stride=nx)

    def roll(value, shift):
        shift = shift % ny
        return value if shift == 0 else pltpu.roll(value, shift, 1)

    def exists(dx, dy):
        ok = my_x >= 0
        if dx != 0:
            ok = (my_x + dx >= 0) & (my_x + dx < size_x)
        if dy != 0:
            ok = ok & (my_y + dy >= 0) & (my_y + dy < size_y)
        return ok

    ext[...] = jnp.zeros_like(ext)
    edge_land[...] = jnp.zeros_like(edge_land)
    mat_ext[...] = jnp.zeros_like(mat_ext)
    mat_land[...] = jnp.zeros_like(mat_land)
    pack_land[...] = jnp.zeros_like(pack_land)
    mask_land[...] = jnp.zeros_like(mask_land)

    barrier = pltpu.get_barrier_semaphore()
    for dx, dy in DIRECTIONS:
        @pl.when(exists(dx, dy))
        def _(dx=dx, dy=dy):
            pl.semaphore_signal(
                barrier, inc=1, device_id=(my_x + dx, my_y + dy), device_id_type=MESH
            )

    def pack_edges(fields, target):
        up = jnp.zeros((rows, ny), jnp.float32)
        down = jnp.zeros((rows, ny), jnp.float32)
        for f, value in enumerate(fields):
            up = jnp.where(lane // 4 == ny // 4 - 1 - f, roll(value, -4 * f), up)
            down = jnp.where(lane // 4 == f, roll(value, 4 * f), down)
        target[0] = up
        target[1] = down

    def halo_copies(whole, sent, land, ssem, rsem):
        copies = []
        for index, (dx, dy) in enumerate(DIRECTIONS):
            place = pl.ds((1 - dx) * rows, rows)
            if dy == 0:
                source = whole.at[:, pl.ds(rows, rows), :]
                target = whole.at[:, place, :]
            else:
                side = 0 if dy > 0 else 1
                source = sent.at[side]
                target = land.at[side, place, :]
            copy = pltpu.make_async_remote_copy(
                src_ref=source, dst_ref=target, send_sem=ssem.at[index], recv_sem=rsem.at[index],
                device_id=(my_x + dx, my_y + dy), device_id_type=MESH,
            )
            copies.append((dx, dy, copy))
        return copies

    def mask_copies():
        return [(1, 0, pltpu.make_async_remote_copy(
            src_ref=mask_send, dst_ref=mask_land, send_sem=mx_ssem.at[0], recv_sem=mx_rsem.at[0],
            device_id=(my_x + 1, my_y), device_id_type=MESH,
        ))]

    def pack_copies():
        copies = []
        for index, (dx, dy) in enumerate([(0, 1), (0, -1), (1, 1), (1, -1)]):
            side = 0 if dy > 0 else 1
            copies.append((dx, dy, pltpu.make_async_remote_copy(
                src_ref=pack_send.at[side],
                dst_ref=pack_land.at[side, pl.ds((1 - dx) * rows, rows), :],
                send_sem=pk_ssem.at[index], recv_sem=pk_rsem.at[index],
                device_id=(my_x + dx, my_y + dy), device_id_type=MESH,
            )))
        return copies

    def start(copies):
        for dx, dy, copy in copies:
            pl.when(exists(dx, dy))(copy.start)

    def arrive(copies):
        for dx, dy, copy in copies:
            pl.when(exists(-dx, -dy))(copy.wait_recv)

    def leave(copies):
        for dx, dy, copy in copies:
            pl.when(exists(dx, dy))(copy.wait_send)

    def step_copies(s):
        return halo_copies(ext.at[s], edge_send.at[s], edge_land.at[s], send_sem.at[s], recv_sem.at[s])

    mat_copies = halo_copies(mat_ext, mat_send, mat_land, mat_ssem, mat_rsem)

    for x in range(nx):
        at = pl.ds(rows + x * nz, nz)
        for f in range(3):
            ext[0, f, at, :] = disp_in[f, layer(x), :]
            vel[f, pl.ds(x * nz, nz), :] = vel_in[f, layer(x), :]
        labels = lab_in[layer(x), :]
        modulus = jnp.zeros(labels.shape, jnp.float32)
        limit = jnp.zeros(labels.shape, jnp.float32)
        for material in range(MATS):
            matches = labels == material
            modulus = jnp.where(matches, stiff[material], modulus)
            limit = jnp.where(matches, crit[material], limit)
        mat_ext[0, at, :] = modulus
        mat_ext[1, at, :] = limit
    own = pl.ds(rows, rows)
    pack_edges([mat_ext[f, own, :] for f in range(2)], mat_send)
    pack_edges([ext[0, f, own, :] for f in range(3)], edge_send.at[0])

    neighbours = lax.select(my_x > 0, 1, 0) + lax.select(my_x < size_x - 1, 1, 0) + 1
    neighbours = neighbours * (lax.select(my_y > 0, 1, 0) + lax.select(my_y < size_y - 1, 1, 0) + 1) - 1
    pl.semaphore_wait(barrier, neighbours)
    start(mat_copies)
    start(step_copies(0))

    def mask_row(k, x):
        return nz * (sum(OFFSETS[q][0] for q in range(k)) + x)

    up = jnp.zeros((rows, ny), jnp.float32)
    down = jnp.zeros((rows, ny), jnp.float32)
    for k, d in enumerate(OFFSETS):
        for x in range(nx):
            value = mask_in[k, layer(x), :].astype(jnp.float32)
            mask_ext[k, pl.ds(rows + x * nz, nz), :] = value
            if x >= nx - d[0]:
                mask_send[pl.ds(mask_row(k, x - (nx - d[0])), nz), :] = value
    start(mask_copies())
    for k, d in enumerate(OFFSETS):
        c = d[2]
        if c > 0:
            value = mask_ext[k, own, :]
            up = jnp.where(lane // 4 == SLOT[k], roll(value, c + 4 * SLOT[k]), up)
        elif c < 0:
            value = mask_ext[k, own, :]
            down = jnp.where(lane // 4 == ny // 4 - 1 - SLOT[k], roll(value, c - 4 * SLOT[k]), down)
    pack_send[0] = up
    pack_send[1] = down
    start(pack_copies())

    def shift_fields(source, land, target, count, add_step):
        full = 3 * rows
        lanes = lax.broadcasted_iota(jnp.int32, (full, ny), 1)
        for f in range(count):
            value = source[f]
            high = roll(land[1], -4 * f)
            low = roll(land[0], 4 * f)
            for c in range(-3, 4):
                moved_value = value
                if c > 0:
                    moved_value = roll(jnp.where(lanes < c, high, value), -c)
                elif c < 0:
                    moved_value = roll(jnp.where(lanes >= ny + c, low, value), -c)
                if add_step and f == 2 and c != 0:
                    moved_value = moved_value + float(c)
                target[c + 3, f] = moved_value

    arrive(mat_copies)
    shift_fields(mat_ext, mat_land, mat_moved, 2, False)

    def inside_depth(b):
        return jnp.where((depth + b >= 0) & (depth + b < nz), 1.0, 0.0).astype(jnp.float32)

    def coefficients(number, offset, live):
        a, b, c = offset
        length = math.sqrt(a * a + b * b + c * c)
        at = pl.ds(rows + nz * a + b, rows)
        here, there = mat_ext[0, own, :], mat_moved[c + 3, 0, at, :]
        limit = mat_ext[1, own, :] + mat_moved[c + 3, 1, at, :]
        square = limit * limit * (0.25 * length * length)
        if b != 0:
            live = live * inside_depth(b)
        gain[number] = (here * there) / (here + there) * (square * (2.0 / length**3)) * live
        spread[number] = square

    for number, (k, forward, offset) in enumerate(SHELL):
        if forward:
            coefficients(number, offset, mask_ext[k, own, :])

    arrive(mask_copies())
    arrive(pack_copies())
    for k in range(FLAT, len(OFFSETS)):
        a = OFFSETS[k][0]
        mask_ext[k, pl.ds(0, rows), :] = jnp.zeros((rows, ny), jnp.float32)
        mask_ext[k, pl.ds((nx - a) * nz, a * nz), :] = mask_land[pl.ds(mask_row(k, 0), a * nz), :]
    for k in range(FLAT):
        mask_ext[k, pl.ds(0, rows), :] = jnp.zeros((rows, ny), jnp.float32)
    for number, (k, forward, offset) in enumerate(SHELL):
        if not forward:
            a, b, c = OFFSETS[k]
            at = pl.ds(rows - nz * a - b, rows)
            live = roll(mask_ext[k, at, :], c)
            if c > 0:
                live = jnp.where(lane < c, roll(pack_land[0, at, :], -4 * SLOT[k]), live)
            elif c < 0:
                live = jnp.where(lane >= ny + c, roll(pack_land[1, at, :], 4 * SLOT[k]), live)
            coefficients(number, offset, live)

    def one_step(s, carry):
        arrive(step_copies(s))
        shift_fields(ext.at[s], edge_land.at[s], moved, 3, True)
        here = [ext[s, f, own, :] for f in range(3)]
        force = [jnp.zeros((rows, ny), jnp.float32) for _ in range(3)]
        for number, (k, forward, offset) in enumerate(SHELL):
            a, b, c = offset
            length = math.sqrt(a * a + b * b + c * c)
            at = pl.ds(rows + nz * a + b, rows)
            e = [
                moved[c + 3, 0, at, :] - (here[0] - float(a)),
                moved[c + 3, 1, at, :] - (here[1] - float(b)),
                moved[c + 3, 2, at, :] - here[2],
            ]
            square = jnp.maximum(e[0] * e[0] + e[1] * e[1] + e[2] * e[2], 1e-30)
            t = square * lax.rsqrt(square) - length
            magnitude = gain[number] * t / (spread[number] + t * t)
            force = [force[f] + magnitude * e[f] for f in range(3)]
        fresh = []
        for f in range(3):
            velocity = vel[f] + time_step * force[f]
            vel[f] = velocity
            fresh.append(here[f] + time_step * velocity)

        @pl.when(s < STEPS - 1)
        def _():
            for f in range(3):
                ext[s + 1, f, own, :] = fresh[f]
            pack_edges(fresh, edge_send.at[s + 1])
            start(step_copies(s + 1))

        @pl.when(s == STEPS - 1)
        def _():
            for f in range(3):
                moved[3, f, pl.ds(0, rows), :] = fresh[f]
        return carry

    lax.fori_loop(0, STEPS, one_step, 0)
    for f in range(3):
        for x in range(nx):
            disp_out[f, layer(x), :] = moved[3, f, pl.ds(x * nz, nz), :]
            vel_out[f, layer(x), :] = vel[f, pl.ds(x * nz, nz), :]

    leave(mat_copies)
    leave(mask_copies())
    leave(pack_copies())

    def drain(s, carry):
        leave(step_copies(s))
        return carry

    lax.fori_loop(0, STEPS, drain, 0)


def on_device(displacement, velocity, labels, bond_mask, stiffness, critical):
    nx, nz, ny = labels.shape
    rows = nx * nz
    count = len(SHELL)
    edge_rows = -(-nz * sum(d[0] for d in OFFSETS) // 8) * 8

    def by_depth(value):
        lead = value.shape[:-3]
        order = tuple(range(len(lead))) + tuple(len(lead) + i for i in (1, 0, 2))
        return value.transpose(order).reshape(lead + (rows, ny))

    f32 = jnp.float32
    vmem, smem = pl.BlockSpec(memory_space=pltpu.VMEM), pl.BlockSpec(memory_space=pltpu.SMEM)
    dma = pltpu.SemaphoreType.DMA
    results = pl.pallas_call(
        functools.partial(kernel, (nx, nz, ny)),
        out_shape=[jax.ShapeDtypeStruct((3, rows, ny), f32)] * 2,
        in_specs=[vmem] * 4 + [smem] * 2,
        out_specs=[vmem] * 2,
        scratch_shapes=[
            pltpu.VMEM((STEPS, 3, 3 * rows, ny), f32),
            pltpu.VMEM((STEPS, 2, rows, ny), f32),
            pltpu.VMEM((STEPS, 2, 3 * rows, ny), f32),
            pltpu.VMEM((2, 3 * rows, ny), f32),
            pltpu.VMEM((2, rows, ny), f32),
            pltpu.VMEM((2, 3 * rows, ny), f32),
            pltpu.VMEM((edge_rows, ny), f32),
            pltpu.VMEM((edge_rows, ny), f32),
            pltpu.VMEM((len(OFFSETS), 2 * rows, ny), f32),
            pltpu.VMEM((2, rows, ny), f32),
            pltpu.VMEM((2, 2 * rows, ny), f32),
            pltpu.VMEM((7, 3, 3 * rows, ny), f32),
            pltpu.VMEM((7, 2, 3 * rows, ny), f32),
            pltpu.VMEM((count, rows, ny), f32),
            pltpu.VMEM((count, rows, ny), f32),
            pltpu.VMEM((3, rows, ny), f32),
            dma((STEPS, 8)), dma((STEPS, 8)), dma((8,)), dma((8,)),
            dma((1,)), dma((1,)), dma((4,)), dma((4,)),
        ],
        compiler_params=pltpu.CompilerParams(
            collective_id=0, has_side_effects=True, vmem_limit_bytes=40 * 1024 * 1024
        ),
        name="peridynamics",
    )(
        by_depth(displacement), by_depth(velocity), by_depth(labels), by_depth(bond_mask),
        stiffness, critical,
    )
    return tuple(value.reshape(3, nz, nx, ny).transpose(0, 2, 1, 3) for value in results)


def solution(mesh):
    in_specs = (
        P(None, "wx", None, "ny"),
        P(None, "wx", None, "ny"),
        P("wx", None, "ny"),
        P(None, "wx", None, "ny"),
        P(),
        P(),
    )
    out_specs = (P(None, "wx", None, "ny"), P(None, "wx", None, "ny"))
    return jax.shard_map(
        on_device, mesh=mesh, in_specs=in_specs, out_specs=out_specs, check_vma=False
    )
```

```python
import functools
import math

import jax
import jax.numpy as jnp
from jax import lax
from jax.experimental import pallas as pl
from jax.experimental.pallas import tpu as pltpu
from jax.sharding import PartitionSpec as P

STEPS = 3
MATS = 8
time_step = 0.05
MESH = pl.DeviceIdType.MESH
DIRECTIONS = [(dx, dy) for dx in (-1, 0, 1) for dy in (-1, 0, 1) if (dx, dy) != (0, 0)]


def bond_offsets():
    chosen = []
    for step_x in range(0, 4):
        for step_z in range(-3, 4):
            for step_y in range(-3, 4):
                if step_x * step_x + step_z * step_z + step_y * step_y <= 9:
                    if step_x > 0 or (step_x == 0 and (step_z > 0 or (step_z == 0 and step_y > 0))):
                        chosen.append((step_x, step_z, step_y))
    return chosen


OFFSETS = bond_offsets()
SLOT = {}
for _sign in (1, -1):
    for _k in [k for k, d in enumerate(OFFSETS) if d[2] * _sign > 0]:
        SLOT[_k] = sum(1 for q in SLOT if OFFSETS[q][2] * _sign > 0)
SHELL = sorted(
    [(k, True, d) for k, d in enumerate(OFFSETS)]
    + [(k, False, (-d[0], -d[1], -d[2])) for k, d in enumerate(OFFSETS)],
    key=lambda item: item[2],
)
FLAT = sum(1 for d in OFFSETS if d[0] == 0)


def kernel(
    shape,
    disp_far, vel_far, lab_far, mask_far, stiff, crit,
    disp_out, vel_out,
    disp_in, vel_in, lab_in, mask_in, in_sem,
    ext, edge_send, edge_land, mat_ext, mat_send, mat_land,
    mask_send, mask_land, mask_ext, pack_send, pack_land,
    moved, mat_moved, gain, spread, vel,
    send_sem, recv_sem, mat_ssem, mat_rsem, mx_ssem, mx_rsem, pk_ssem, pk_rsem,
):
    nx, nz, ny = shape
    rows = nx * nz
    size_x, size_y = lax.axis_size("wx"), lax.axis_size("ny")
    my_x, my_y = lax.axis_index("wx"), lax.axis_index("ny")
    lane = lax.broadcasted_iota(jnp.int32, (rows, ny), 1)
    row = lax.broadcasted_iota(jnp.int32, (rows, ny), 0)
    depth = row % nz

    def layer(x):
        return pl.ds(x, nz, stride=nx)

    def roll(value, shift):
        shift = shift % ny
        return value if shift == 0 else pltpu.roll(value, shift, 1)

    def exists(dx, dy):
        ok = my_x >= 0
        if dx != 0:
            ok = (my_x + dx >= 0) & (my_x + dx < size_x)
        if dy != 0:
            ok = ok & (my_y + dy >= 0) & (my_y + dy < size_y)
        return ok

    reads = [
        pltpu.make_async_copy(source, target, in_sem.at[number])
        for number, (source, target) in enumerate(
            [(lab_far, lab_in), (disp_far, disp_in), (vel_far, vel_in), (mask_far, mask_in)]
        )
    ]
    for read in reads:
        read.start()

    ext[...] = jnp.zeros_like(ext)
    edge_land[...] = jnp.zeros_like(edge_land)
    mat_ext[...] = jnp.zeros_like(mat_ext)
    mat_land[...] = jnp.zeros_like(mat_land)
    pack_land[...] = jnp.zeros_like(pack_land)
    mask_land[...] = jnp.zeros_like(mask_land)

    barrier = pltpu.get_barrier_semaphore()
    for dx, dy in DIRECTIONS:
        @pl.when(exists(dx, dy))
        def _(dx=dx, dy=dy):
            pl.semaphore_signal(
                barrier, inc=1, device_id=(my_x + dx, my_y + dy), device_id_type=MESH
            )

    def pack_edges(fields, target):
        up = jnp.zeros((rows, ny), jnp.float32)
        down = jnp.zeros((rows, ny), jnp.float32)
        for f, value in enumerate(fields):
            up = jnp.where(lane // 4 == ny // 4 - 1 - f, roll(value, -4 * f), up)
            down = jnp.where(lane // 4 == f, roll(value, 4 * f), down)
        target[0] = up
        target[1] = down

    def halo_copies(whole, sent, land, ssem, rsem):
        copies = []
        for index, (dx, dy) in enumerate(DIRECTIONS):
            place = pl.ds((1 - dx) * rows, rows)
            if dy == 0:
                source = whole.at[:, pl.ds(rows, rows), :]
                target = whole.at[:, place, :]
            else:
                side = 0 if dy > 0 else 1
                source = sent.at[side]
                target = land.at[side, place, :]
            copy = pltpu.make_async_remote_copy(
                src_ref=source, dst_ref=target, send_sem=ssem.at[index], recv_sem=rsem.at[index],
                device_id=(my_x + dx, my_y + dy), device_id_type=MESH,
            )
            copies.append((dx, dy, copy))
        return copies

    def mask_copies():
        return [(1, 0, pltpu.make_async_remote_copy(
            src_ref=mask_send, dst_ref=mask_land, send_sem=mx_ssem.at[0], recv_sem=mx_rsem.at[0],
            device_id=(my_x + 1, my_y), device_id_type=MESH,
        ))]

    def pack_copies():
        copies = []
        for index, (dx, dy) in enumerate([(0, 1), (0, -1), (1, 1), (1, -1)]):
            side = 0 if dy > 0 else 1
            copies.append((dx, dy, pltpu.make_async_remote_copy(
                src_ref=pack_send.at[side],
                dst_ref=pack_land.at[side, pl.ds((1 - dx) * rows, rows), :],
                send_sem=pk_ssem.at[index], recv_sem=pk_rsem.at[index],
                device_id=(my_x + dx, my_y + dy), device_id_type=MESH,
            )))
        return copies

    def start(copies):
        for dx, dy, copy in copies:
            pl.when(exists(dx, dy))(copy.start)

    def arrive(copies):
        for dx, dy, copy in copies:
            pl.when(exists(-dx, -dy))(copy.wait_recv)

    def leave(copies):
        for dx, dy, copy in copies:
            pl.when(exists(dx, dy))(copy.wait_send)

    def step_copies(s):
        return halo_copies(ext.at[s], edge_send.at[s], edge_land.at[s], send_sem.at[s], recv_sem.at[s])

    mat_copies = halo_copies(mat_ext, mat_send, mat_land, mat_ssem, mat_rsem)

    for read in reads[:3]:
        read.wait()
    for x in range(nx):
        at = pl.ds(rows + x * nz, nz)
        for f in range(3):
            ext[0, f, at, :] = disp_in[f, layer(x), :]
            vel[f, pl.ds(x * nz, nz), :] = vel_in[f, layer(x), :]
        labels = lab_in[layer(x), :]
        modulus = jnp.zeros(labels.shape, jnp.float32)
        limit = jnp.zeros(labels.shape, jnp.float32)
        for material in range(MATS):
            matches = labels == material
            modulus = jnp.where(matches, stiff[material], modulus)
            limit = jnp.where(matches, crit[material], limit)
        mat_ext[0, at, :] = modulus
        mat_ext[1, at, :] = limit
    own = pl.ds(rows, rows)
    pack_edges([mat_ext[f, own, :] for f in range(2)], mat_send)
    pack_edges([ext[0, f, own, :] for f in range(3)], edge_send.at[0])

    neighbours = lax.select(my_x > 0, 1, 0) + lax.select(my_x < size_x - 1, 1, 0) + 1
    neighbours = neighbours * (lax.select(my_y > 0, 1, 0) + lax.select(my_y < size_y - 1, 1, 0) + 1) - 1
    pl.semaphore_wait(barrier, neighbours)
    start(mat_copies)
    start(step_copies(0))

    reads[3].wait()

    def mask_row(k, x):
        return nz * (sum(OFFSETS[q][0] for q in range(k)) + x)

    up = jnp.zeros((rows, ny), jnp.float32)
    down = jnp.zeros((rows, ny), jnp.float32)
    for k, d in enumerate(OFFSETS):
        for x in range(nx):
            value = mask_in[k, layer(x), :].astype(jnp.float32)
            mask_ext[k, pl.ds(rows + x * nz, nz), :] = value
            if x >= nx - d[0]:
                mask_send[pl.ds(mask_row(k, x - (nx - d[0])), nz), :] = value
    start(mask_copies())
    for k, d in enumerate(OFFSETS):
        c = d[2]
        if c > 0:
            value = mask_ext[k, own, :]
            up = jnp.where(lane // 4 == SLOT[k], roll(value, c + 4 * SLOT[k]), up)
        elif c < 0:
            value = mask_ext[k, own, :]
            down = jnp.where(lane // 4 == ny // 4 - 1 - SLOT[k], roll(value, c - 4 * SLOT[k]), down)
    pack_send[0] = up
    pack_send[1] = down
    start(pack_copies())

    def shift_fields(source, land, target, count, add_step):
        full = 3 * rows
        lanes = lax.broadcasted_iota(jnp.int32, (full, ny), 1)
        for f in range(count):
            value = source[f]
            high = roll(land[1], -4 * f)
            low = roll(land[0], 4 * f)
            for c in range(-3, 4):
                moved_value = value
                if c > 0:
                    moved_value = roll(jnp.where(lanes < c, high, value), -c)
                elif c < 0:
                    moved_value = roll(jnp.where(lanes >= ny + c, low, value), -c)
                if add_step and f == 2 and c != 0:
                    moved_value = moved_value + float(c)
                target[c + 3, f] = moved_value

    arrive(mat_copies)
    shift_fields(mat_ext, mat_land, mat_moved, 2, False)

    def inside_depth(b):
        return jnp.where((depth + b >= 0) & (depth + b < nz), 1.0, 0.0).astype(jnp.float32)

    def coefficients(number, offset, live):
        a, b, c = offset
        length = math.sqrt(a * a + b * b + c * c)
        at = pl.ds(rows + nz * a + b, rows)
        here, there = mat_ext[0, own, :], mat_moved[c + 3, 0, at, :]
        limit = mat_ext[1, own, :] + mat_moved[c + 3, 1, at, :]
        square = limit * limit * (0.25 * length * length)
        if b != 0:
            live = live * inside_depth(b)
        gain[number] = (here * there) / (here + there) * (square * (2.0 / length**3)) * live
        spread[number] = square

    for number, (k, forward, offset) in enumerate(SHELL):
        if forward:
            coefficients(number, offset, mask_ext[k, own, :])

    arrive(mask_copies())
    arrive(pack_copies())
    for k in range(FLAT, len(OFFSETS)):
        a = OFFSETS[k][0]
        mask_ext[k, pl.ds(0, rows), :] = jnp.zeros((rows, ny), jnp.float32)
        mask_ext[k, pl.ds((nx - a) * nz, a * nz), :] = mask_land[pl.ds(mask_row(k, 0), a * nz), :]
    for k in range(FLAT):
        mask_ext[k, pl.ds(0, rows), :] = jnp.zeros((rows, ny), jnp.float32)
    for number, (k, forward, offset) in enumerate(SHELL):
        if not forward:
            a, b, c = OFFSETS[k]
            at = pl.ds(rows - nz * a - b, rows)
            live = roll(mask_ext[k, at, :], c)
            if c > 0:
                live = jnp.where(lane < c, roll(pack_land[0, at, :], -4 * SLOT[k]), live)
            elif c < 0:
                live = jnp.where(lane >= ny + c, roll(pack_land[1, at, :], 4 * SLOT[k]), live)
            coefficients(number, offset, live)

    def one_step(s, carry):
        arrive(step_copies(s))
        shift_fields(ext.at[s], edge_land.at[s], moved, 3, True)
        here = [ext[s, f, own, :] for f in range(3)]
        force = [jnp.zeros((rows, ny), jnp.float32) for _ in range(3)]
        for number, (k, forward, offset) in enumerate(SHELL):
            a, b, c = offset
            length = math.sqrt(a * a + b * b + c * c)
            at = pl.ds(rows + nz * a + b, rows)
            e = [
                moved[c + 3, 0, at, :] - (here[0] - float(a)),
                moved[c + 3, 1, at, :] - (here[1] - float(b)),
                moved[c + 3, 2, at, :] - here[2],
            ]
            square = jnp.maximum(e[0] * e[0] + e[1] * e[1] + e[2] * e[2], 1e-30)
            t = square * lax.rsqrt(square) - length
            magnitude = gain[number] * t / (spread[number] + t * t)
            force = [force[f] + magnitude * e[f] for f in range(3)]
        fresh = []
        for f in range(3):
            velocity = vel[f] + time_step * force[f]
            vel[f] = velocity
            fresh.append(here[f] + time_step * velocity)

        @pl.when(s < STEPS - 1)
        def _():
            for f in range(3):
                ext[s + 1, f, own, :] = fresh[f]
            pack_edges(fresh, edge_send.at[s + 1])
            start(step_copies(s + 1))

        @pl.when(s == STEPS - 1)
        def _():
            for f in range(3):
                moved[3, f, pl.ds(0, rows), :] = fresh[f]
        return carry

    lax.fori_loop(0, STEPS, one_step, 0)
    for f in range(3):
        for x in range(nx):
            disp_out[f, layer(x), :] = moved[3, f, pl.ds(x * nz, nz), :]
            vel_out[f, layer(x), :] = vel[f, pl.ds(x * nz, nz), :]

    leave(mat_copies)
    leave(mask_copies())
    leave(pack_copies())

    def drain(s, carry):
        leave(step_copies(s))
        return carry

    lax.fori_loop(0, STEPS, drain, 0)


def on_device(displacement, velocity, labels, bond_mask, stiffness, critical):
    nx, nz, ny = labels.shape
    rows = nx * nz
    count = len(SHELL)
    edge_rows = -(-nz * sum(d[0] for d in OFFSETS) // 8) * 8

    def by_depth(value):
        lead = value.shape[:-3]
        order = tuple(range(len(lead))) + tuple(len(lead) + i for i in (1, 0, 2))
        return value.transpose(order).reshape(lead + (rows, ny))

    f32 = jnp.float32
    vmem, smem = pl.BlockSpec(memory_space=pltpu.VMEM), pl.BlockSpec(memory_space=pltpu.SMEM)
    dma = pltpu.SemaphoreType.DMA
    results = pl.pallas_call(
        functools.partial(kernel, (nx, nz, ny)),
        out_shape=[jax.ShapeDtypeStruct((3, rows, ny), f32)] * 2,
        in_specs=[pl.BlockSpec(memory_space=pltpu.HBM)] * 4 + [smem] * 2,
        out_specs=[vmem] * 2,
        scratch_shapes=[
            pltpu.VMEM((3, rows, ny), f32),
            pltpu.VMEM((3, rows, ny), f32),
            pltpu.VMEM((rows, ny), jnp.int32),
            pltpu.VMEM((len(OFFSETS), rows, ny), jnp.int32),
            dma((4,)),
            pltpu.VMEM((STEPS, 3, 3 * rows, ny), f32),
            pltpu.VMEM((STEPS, 2, rows, ny), f32),
            pltpu.VMEM((STEPS, 2, 3 * rows, ny), f32),
            pltpu.VMEM((2, 3 * rows, ny), f32),
            pltpu.VMEM((2, rows, ny), f32),
            pltpu.VMEM((2, 3 * rows, ny), f32),
            pltpu.VMEM((edge_rows, ny), f32),
            pltpu.VMEM((edge_rows, ny), f32),
            pltpu.VMEM((len(OFFSETS), 2 * rows, ny), f32),
            pltpu.VMEM((2, rows, ny), f32),
            pltpu.VMEM((2, 2 * rows, ny), f32),
            pltpu.VMEM((7, 3, 3 * rows, ny), f32),
            pltpu.VMEM((7, 2, 3 * rows, ny), f32),
            pltpu.VMEM((count, rows, ny), f32),
            pltpu.VMEM((count, rows, ny), f32),
            pltpu.VMEM((3, rows, ny), f32),
            dma((STEPS, 8)), dma((STEPS, 8)), dma((8,)), dma((8,)),
            dma((1,)), dma((1,)), dma((4,)), dma((4,)),
        ],
        compiler_params=pltpu.CompilerParams(
            collective_id=0, has_side_effects=True, vmem_limit_bytes=63 * 1024 * 1024 + 960 * 1024
        ),
        name="peridynamics",
    )(
        by_depth(displacement), by_depth(velocity), by_depth(labels), by_depth(bond_mask),
        stiffness, critical,
    )
    return tuple(value.reshape(3, nz, nx, ny).transpose(0, 2, 1, 3) for value in results)


def solution(mesh):
    in_specs = (
        P(None, "wx", None, "ny"),
        P(None, "wx", None, "ny"),
        P("wx", None, "ny"),
        P(None, "wx", None, "ny"),
        P(),
        P(),
    )
    out_specs = (P(None, "wx", None, "ny"), P(None, "wx", None, "ny"))
    return jax.shard_map(
        on_device, mesh=mesh, in_specs=in_specs, out_specs=out_specs, check_vma=False
    )
```

```python
import functools
import math

import jax
import jax.numpy as jnp
from jax import lax
from jax.experimental import pallas as pl
from jax.experimental.pallas import tpu as pltpu
from jax.sharding import PartitionSpec as P

STEPS = 3
MATS = 8
time_step = 0.05
MESH = pl.DeviceIdType.MESH
DIRECTIONS = [(dx, dy) for dx in (-1, 0, 1) for dy in (-1, 0, 1) if (dx, dy) != (0, 0)]


def bond_offsets():
    chosen = []
    for step_x in range(0, 4):
        for step_z in range(-3, 4):
            for step_y in range(-3, 4):
                if step_x * step_x + step_z * step_z + step_y * step_y <= 9:
                    if step_x > 0 or (step_x == 0 and (step_z > 0 or (step_z == 0 and step_y > 0))):
                        chosen.append((step_x, step_z, step_y))
    return chosen


OFFSETS = bond_offsets()
SLOT = {}
for _sign in (1, -1):
    for _k in [k for k, d in enumerate(OFFSETS) if d[2] * _sign > 0]:
        SLOT[_k] = sum(1 for q in SLOT if OFFSETS[q][2] * _sign > 0)
SHELL = sorted(
    [(k, True, d) for k, d in enumerate(OFFSETS)]
    + [(k, False, (-d[0], -d[1], -d[2])) for k, d in enumerate(OFFSETS)],
    key=lambda item: item[2],
)
FLAT = sum(1 for d in OFFSETS if d[0] == 0)


def kernel(
    shape,
    disp_far, vel_far, lab_far, mask_far, stiff, crit,
    disp_out, vel_out,
    disp_in, vel_in, lab_in, mask_in, in_sem,
    ext, edge_send, edge_land, mat_ext, mat_send, mat_land,
    mask_send, mask_land, mask_ext, pack_send, pack_land,
    moved, mat_moved, gain, spread, vel,
    send_sem, recv_sem, mat_ssem, mat_rsem, mx_ssem, mx_rsem, pk_ssem, pk_rsem,
):
    nx, nz, ny = shape
    rows = nx * nz
    size_x, size_y = lax.axis_size("wx"), lax.axis_size("ny")
    my_x, my_y = lax.axis_index("wx"), lax.axis_index("ny")
    lane = lax.broadcasted_iota(jnp.int32, (rows, ny), 1)
    row = lax.broadcasted_iota(jnp.int32, (rows, ny), 0)
    depth = row % nz

    def layer(x):
        return pl.ds(x, nz, stride=nx)

    def roll(value, shift):
        shift = shift % ny
        return value if shift == 0 else pltpu.roll(value, shift, 1)

    def exists(dx, dy):
        ok = my_x >= 0
        if dx != 0:
            ok = (my_x + dx >= 0) & (my_x + dx < size_x)
        if dy != 0:
            ok = ok & (my_y + dy >= 0) & (my_y + dy < size_y)
        return ok

    reads = [
        pltpu.make_async_copy(source, target, in_sem.at[number])
        for number, (source, target) in enumerate(
            [(lab_far, lab_in), (disp_far, disp_in), (vel_far, vel_in), (mask_far, mask_in)]
        )
    ]
    for read in reads:
        read.start()

    ext[...] = jnp.zeros_like(ext)
    edge_land[...] = jnp.zeros_like(edge_land)
    mat_ext[...] = jnp.zeros_like(mat_ext)
    mat_land[...] = jnp.zeros_like(mat_land)
    pack_land[...] = jnp.zeros_like(pack_land)
    mask_land[...] = jnp.zeros_like(mask_land)

    barrier = pltpu.get_barrier_semaphore()
    for dx, dy in DIRECTIONS:
        @pl.when(exists(dx, dy))
        def _(dx=dx, dy=dy):
            pl.semaphore_signal(
                barrier, inc=1, device_id=(my_x + dx, my_y + dy), device_id_type=MESH
            )

    def pack_edges(fields, target):
        up = jnp.zeros((rows, ny), jnp.float32)
        down = jnp.zeros((rows, ny), jnp.float32)
        for f, value in enumerate(fields):
            up = jnp.where(lane // 4 == ny // 4 - 1 - f, roll(value, -4 * f), up)
            down = jnp.where(lane // 4 == f, roll(value, 4 * f), down)
        target[0] = up
        target[1] = down

    def halo_copies(whole, sent, land, ssem, rsem):
        copies = []
        for index, (dx, dy) in enumerate(DIRECTIONS):
            place = pl.ds((1 - dx) * rows, rows)
            if dy == 0:
                source = whole.at[:, pl.ds(rows, rows), :]
                target = whole.at[:, place, :]
            else:
                side = 0 if dy > 0 else 1
                source = sent.at[side]
                target = land.at[side, place, :]
            copy = pltpu.make_async_remote_copy(
                src_ref=source, dst_ref=target, send_sem=ssem.at[index], recv_sem=rsem.at[index],
                device_id=(my_x + dx, my_y + dy), device_id_type=MESH,
            )
            copies.append((dx, dy, copy))
        return copies

    def mask_copies():
        return [(1, 0, pltpu.make_async_remote_copy(
            src_ref=mask_send, dst_ref=mask_land, send_sem=mx_ssem.at[0], recv_sem=mx_rsem.at[0],
            device_id=(my_x + 1, my_y), device_id_type=MESH,
        ))]

    def pack_copies():
        copies = []
        for index, (dx, dy) in enumerate([(0, 1), (0, -1), (1, 1), (1, -1)]):
            side = 0 if dy > 0 else 1
            copies.append((dx, dy, pltpu.make_async_remote_copy(
                src_ref=pack_send.at[side],
                dst_ref=pack_land.at[side, pl.ds((1 - dx) * rows, rows), :],
                send_sem=pk_ssem.at[index], recv_sem=pk_rsem.at[index],
                device_id=(my_x + dx, my_y + dy), device_id_type=MESH,
            )))
        return copies

    def start(copies):
        for dx, dy, copy in copies:
            pl.when(exists(dx, dy))(copy.start)

    def arrive(copies):
        for dx, dy, copy in copies:
            pl.when(exists(-dx, -dy))(copy.wait_recv)

    def leave(copies):
        for dx, dy, copy in copies:
            pl.when(exists(dx, dy))(copy.wait_send)

    def step_copies(s):
        return halo_copies(ext.at[s], edge_send.at[s], edge_land.at[s], send_sem.at[s], recv_sem.at[s])

    mat_copies = halo_copies(mat_ext, mat_send, mat_land, mat_ssem, mat_rsem)

    for read in reads[:3]:
        read.wait()
    for x in range(nx):
        at = pl.ds(rows + x * nz, nz)
        for f in range(3):
            ext[0, f, at, :] = disp_in[f, layer(x), :]
            vel[f, pl.ds(x * nz, nz), :] = vel_in[f, layer(x), :]
        labels = lab_in[layer(x), :]
        modulus = jnp.zeros(labels.shape, jnp.float32)
        limit = jnp.zeros(labels.shape, jnp.float32)
        for material in range(MATS):
            matches = labels == material
            modulus = jnp.where(matches, stiff[material], modulus)
            limit = jnp.where(matches, crit[material], limit)
        mat_ext[0, at, :] = modulus
        mat_ext[1, at, :] = limit
    own = pl.ds(rows, rows)
    pack_edges([mat_ext[f, own, :] for f in range(2)], mat_send)
    pack_edges([ext[0, f, own, :] for f in range(3)], edge_send.at[0])

    reads[3].wait()

    def mask_row(k, x):
        return nz * (sum(OFFSETS[q][0] for q in range(k)) + x)

    up = jnp.zeros((rows, ny), jnp.float32)
    down = jnp.zeros((rows, ny), jnp.float32)
    for k, d in enumerate(OFFSETS):
        for x in range(nx):
            value = mask_in[k, layer(x), :].astype(jnp.float32)
            mask_ext[k, pl.ds(rows + x * nz, nz), :] = value
            if x >= nx - d[0]:
                mask_send[pl.ds(mask_row(k, x - (nx - d[0])), nz), :] = value
    for k, d in enumerate(OFFSETS):
        c = d[2]
        if c > 0:
            value = mask_ext[k, own, :]
            up = jnp.where(lane // 4 == SLOT[k], roll(value, c + 4 * SLOT[k]), up)
        elif c < 0:
            value = mask_ext[k, own, :]
            down = jnp.where(lane // 4 == ny // 4 - 1 - SLOT[k], roll(value, c - 4 * SLOT[k]), down)
    pack_send[0] = up
    pack_send[1] = down

    neighbours = lax.select(my_x > 0, 1, 0) + lax.select(my_x < size_x - 1, 1, 0) + 1
    neighbours = neighbours * (lax.select(my_y > 0, 1, 0) + lax.select(my_y < size_y - 1, 1, 0) + 1) - 1
    pl.semaphore_wait(barrier, neighbours)
    start(mask_copies())
    start(mat_copies)
    start(pack_copies())
    start(step_copies(0))

    def shift_fields(source, land, target, count, add_step):
        full = 3 * rows
        lanes = lax.broadcasted_iota(jnp.int32, (full, ny), 1)
        for f in range(count):
            value = source[f]
            high = roll(land[1], -4 * f)
            low = roll(land[0], 4 * f)
            for c in range(-3, 4):
                moved_value = value
                if c > 0:
                    moved_value = roll(jnp.where(lanes < c, high, value), -c)
                elif c < 0:
                    moved_value = roll(jnp.where(lanes >= ny + c, low, value), -c)
                if add_step and f == 2 and c != 0:
                    moved_value = moved_value + float(c)
                target[c + 3, f] = moved_value

    arrive(mat_copies)
    shift_fields(mat_ext, mat_land, mat_moved, 2, False)

    def inside_depth(b):
        return jnp.where((depth + b >= 0) & (depth + b < nz), 1.0, 0.0).astype(jnp.float32)

    def coefficients(number, offset, live):
        a, b, c = offset
        length = math.sqrt(a * a + b * b + c * c)
        at = pl.ds(rows + nz * a + b, rows)
        here, there = mat_ext[0, own, :], mat_moved[c + 3, 0, at, :]
        limit = mat_ext[1, own, :] + mat_moved[c + 3, 1, at, :]
        square = limit * limit * (0.25 * length * length)
        if b != 0:
            live = live * inside_depth(b)
        gain[number] = (here * there) / (here + there) * (square * (2.0 / length**3)) * live
        spread[number] = square

    for number, (k, forward, offset) in enumerate(SHELL):
        if forward:
            coefficients(number, offset, mask_ext[k, own, :])

    arrive(mask_copies())
    arrive(pack_copies())
    for k in range(FLAT, len(OFFSETS)):
        a = OFFSETS[k][0]
        mask_ext[k, pl.ds(0, rows), :] = jnp.zeros((rows, ny), jnp.float32)
        mask_ext[k, pl.ds((nx - a) * nz, a * nz), :] = mask_land[pl.ds(mask_row(k, 0), a * nz), :]
    for k in range(FLAT):
        mask_ext[k, pl.ds(0, rows), :] = jnp.zeros((rows, ny), jnp.float32)
    for number, (k, forward, offset) in enumerate(SHELL):
        if not forward:
            a, b, c = OFFSETS[k]
            at = pl.ds(rows - nz * a - b, rows)
            live = roll(mask_ext[k, at, :], c)
            if c > 0:
                live = jnp.where(lane < c, roll(pack_land[0, at, :], -4 * SLOT[k]), live)
            elif c < 0:
                live = jnp.where(lane >= ny + c, roll(pack_land[1, at, :], 4 * SLOT[k]), live)
            coefficients(number, offset, live)

    def one_step(s, carry):
        arrive(step_copies(s))
        shift_fields(ext.at[s], edge_land.at[s], moved, 3, True)
        here = [ext[s, f, own, :] for f in range(3)]
        force = [jnp.zeros((rows, ny), jnp.float32) for _ in range(3)]
        for number, (k, forward, offset) in enumerate(SHELL):
            a, b, c = offset
            length = math.sqrt(a * a + b * b + c * c)
            at = pl.ds(rows + nz * a + b, rows)
            e = [
                moved[c + 3, 0, at, :] - (here[0] - float(a)),
                moved[c + 3, 1, at, :] - (here[1] - float(b)),
                moved[c + 3, 2, at, :] - here[2],
            ]
            square = jnp.maximum(e[0] * e[0] + e[1] * e[1] + e[2] * e[2], 1e-30)
            t = square * lax.rsqrt(square) - length
            magnitude = gain[number] * t / (spread[number] + t * t)
            force = [force[f] + magnitude * e[f] for f in range(3)]
        fresh = []
        for f in range(3):
            velocity = vel[f] + time_step * force[f]
            vel[f] = velocity
            fresh.append(here[f] + time_step * velocity)

        @pl.when(s < STEPS - 1)
        def _():
            for f in range(3):
                ext[s + 1, f, own, :] = fresh[f]
            pack_edges(fresh, edge_send.at[s + 1])
            start(step_copies(s + 1))

        @pl.when(s == STEPS - 1)
        def _():
            for f in range(3):
                moved[3, f, pl.ds(0, rows), :] = fresh[f]
        return carry

    lax.fori_loop(0, STEPS, one_step, 0)
    for f in range(3):
        for x in range(nx):
            disp_out[f, layer(x), :] = moved[3, f, pl.ds(x * nz, nz), :]
            vel_out[f, layer(x), :] = vel[f, pl.ds(x * nz, nz), :]

    leave(mat_copies)
    leave(mask_copies())
    leave(pack_copies())

    def drain(s, carry):
        leave(step_copies(s))
        return carry

    lax.fori_loop(0, STEPS, drain, 0)


def on_device(displacement, velocity, labels, bond_mask, stiffness, critical):
    nx, nz, ny = labels.shape
    rows = nx * nz
    count = len(SHELL)
    edge_rows = -(-nz * sum(d[0] for d in OFFSETS) // 8) * 8

    def by_depth(value):
        lead = value.shape[:-3]
        order = tuple(range(len(lead))) + tuple(len(lead) + i for i in (1, 0, 2))
        return value.transpose(order).reshape(lead + (rows, ny))

    f32 = jnp.float32
    vmem, smem = pl.BlockSpec(memory_space=pltpu.VMEM), pl.BlockSpec(memory_space=pltpu.SMEM)
    dma = pltpu.SemaphoreType.DMA
    results = pl.pallas_call(
        functools.partial(kernel, (nx, nz, ny)),
        out_shape=[jax.ShapeDtypeStruct((3, rows, ny), f32)] * 2,
        in_specs=[pl.BlockSpec(memory_space=pltpu.HBM)] * 4 + [smem] * 2,
        out_specs=[vmem] * 2,
        scratch_shapes=[
            pltpu.VMEM((3, rows, ny), f32),
            pltpu.VMEM((3, rows, ny), f32),
            pltpu.VMEM((rows, ny), jnp.int32),
            pltpu.VMEM((len(OFFSETS), rows, ny), jnp.int32),
            dma((4,)),
            pltpu.VMEM((STEPS, 3, 3 * rows, ny), f32),
            pltpu.VMEM((STEPS, 2, rows, ny), f32),
            pltpu.VMEM((STEPS, 2, 3 * rows, ny), f32),
            pltpu.VMEM((2, 3 * rows, ny), f32),
            pltpu.VMEM((2, rows, ny), f32),
            pltpu.VMEM((2, 3 * rows, ny), f32),
            pltpu.VMEM((edge_rows, ny), f32),
            pltpu.VMEM((edge_rows, ny), f32),
            pltpu.VMEM((len(OFFSETS), 2 * rows, ny), f32),
            pltpu.VMEM((2, rows, ny), f32),
            pltpu.VMEM((2, 2 * rows, ny), f32),
            pltpu.VMEM((7, 3, 3 * rows, ny), f32),
            pltpu.VMEM((7, 2, 3 * rows, ny), f32),
            pltpu.VMEM((count, rows, ny), f32),
            pltpu.VMEM((count, rows, ny), f32),
            pltpu.VMEM((3, rows, ny), f32),
            dma((STEPS, 8)), dma((STEPS, 8)), dma((8,)), dma((8,)),
            dma((1,)), dma((1,)), dma((4,)), dma((4,)),
        ],
        compiler_params=pltpu.CompilerParams(
            collective_id=0, has_side_effects=True, vmem_limit_bytes=63 * 1024 * 1024 + 960 * 1024
        ),
        name="peridynamics",
    )(
        by_depth(displacement), by_depth(velocity), by_depth(labels), by_depth(bond_mask),
        stiffness, critical,
    )
    return tuple(value.reshape(3, nz, nx, ny).transpose(0, 2, 1, 3) for value in results)


def solution(mesh):
    in_specs = (
        P(None, "wx", None, "ny"),
        P(None, "wx", None, "ny"),
        P("wx", None, "ny"),
        P(None, "wx", None, "ny"),
        P(),
        P(),
    )
    out_specs = (P(None, "wx", None, "ny"), P(None, "wx", None, "ny"))
    return jax.shard_map(
        on_device, mesh=mesh, in_specs=in_specs, out_specs=out_specs, check_vma=False
    )
```

```python
import functools
import math

import jax
import jax.numpy as jnp
from jax import lax
from jax.experimental import pallas as pl
from jax.experimental.pallas import tpu as pltpu
from jax.sharding import PartitionSpec as P

STEPS = 3
MATS = 8
time_step = 0.05
MESH = pl.DeviceIdType.MESH
DIRECTIONS = [(dx, dy) for dx in (-1, 0, 1) for dy in (-1, 0, 1) if (dx, dy) != (0, 0)]
DIRECTIONS.sort(key=lambda d: -abs(d[0]) - abs(d[1]))


def bond_offsets():
    chosen = []
    for step_x in range(0, 4):
        for step_z in range(-3, 4):
            for step_y in range(-3, 4):
                if step_x * step_x + step_z * step_z + step_y * step_y <= 9:
                    if step_x > 0 or (step_x == 0 and (step_z > 0 or (step_z == 0 and step_y > 0))):
                        chosen.append((step_x, step_z, step_y))
    return chosen


OFFSETS = bond_offsets()
SLOT = {}
for _sign in (1, -1):
    for _k in [k for k, d in enumerate(OFFSETS) if d[2] * _sign > 0]:
        SLOT[_k] = sum(1 for q in SLOT if OFFSETS[q][2] * _sign > 0)
SHELL = sorted(
    [(k, True, d) for k, d in enumerate(OFFSETS)]
    + [(k, False, (-d[0], -d[1], -d[2])) for k, d in enumerate(OFFSETS)],
    key=lambda item: item[2],
)
FLAT = sum(1 for d in OFFSETS if d[0] == 0)


def kernel(
    shape,
    disp_far, vel_far, lab_far, mask_far, stiff, crit,
    disp_out, vel_out,
    disp_in, vel_in, lab_in, mask_in, in_sem,
    ext, edge_send, edge_land, mat_ext, mat_send, mat_land,
    mask_send, mask_land, mask_ext, pack_send, pack_land,
    moved, mat_moved, gain, spread, vel,
    send_sem, recv_sem, mat_ssem, mat_rsem, mx_ssem, mx_rsem, pk_ssem, pk_rsem,
):
    nx, nz, ny = shape
    rows = nx * nz
    size_x, size_y = lax.axis_size("wx"), lax.axis_size("ny")
    my_x, my_y = lax.axis_index("wx"), lax.axis_index("ny")
    lane = lax.broadcasted_iota(jnp.int32, (rows, ny), 1)
    row = lax.broadcasted_iota(jnp.int32, (rows, ny), 0)
    depth = row % nz

    def layer(x):
        return pl.ds(x, nz, stride=nx)

    def roll(value, shift):
        shift = shift % ny
        return value if shift == 0 else pltpu.roll(value, shift, 1)

    def exists(dx, dy):
        ok = my_x >= 0
        if dx != 0:
            ok = (my_x + dx >= 0) & (my_x + dx < size_x)
        if dy != 0:
            ok = ok & (my_y + dy >= 0) & (my_y + dy < size_y)
        return ok

    reads = [
        pltpu.make_async_copy(source, target, in_sem.at[number])
        for number, (source, target) in enumerate(
            [(lab_far, lab_in), (disp_far, disp_in), (vel_far, vel_in), (mask_far, mask_in)]
        )
    ]
    for read in reads:
        read.start()

    ext[...] = jnp.zeros_like(ext)
    edge_land[...] = jnp.zeros_like(edge_land)
    mat_ext[...] = jnp.zeros_like(mat_ext)
    mat_land[...] = jnp.zeros_like(mat_land)
    pack_land[...] = jnp.zeros_like(pack_land)
    mask_land[...] = jnp.zeros_like(mask_land)

    barrier = pltpu.get_barrier_semaphore()
    for dx, dy in DIRECTIONS:
        @pl.when(exists(dx, dy))
        def _(dx=dx, dy=dy):
            pl.semaphore_signal(
                barrier, inc=1, device_id=(my_x + dx, my_y + dy), device_id_type=MESH
            )

    def pack_edges(fields, target):
        up = jnp.zeros((rows, ny), jnp.float32)
        down = jnp.zeros((rows, ny), jnp.float32)
        for f, value in enumerate(fields):
            up = jnp.where(lane // 4 == ny // 4 - 1 - f, roll(value, -4 * f), up)
            down = jnp.where(lane // 4 == f, roll(value, 4 * f), down)
        target[0] = up
        target[1] = down

    def halo_copies(whole, sent, land, ssem, rsem):
        copies = []
        for index, (dx, dy) in enumerate(DIRECTIONS):
            place = pl.ds((1 - dx) * rows, rows)
            if dy == 0:
                source = whole.at[:, pl.ds(rows, rows), :]
                target = whole.at[:, place, :]
            else:
                side = 0 if dy > 0 else 1
                source = sent.at[side]
                target = land.at[side, place, :]
            copy = pltpu.make_async_remote_copy(
                src_ref=source, dst_ref=target, send_sem=ssem.at[index], recv_sem=rsem.at[index],
                device_id=(my_x + dx, my_y + dy), device_id_type=MESH,
            )
            copies.append((dx, dy, copy))
        return copies

    def mask_copies():
        return [(1, 0, pltpu.make_async_remote_copy(
            src_ref=mask_send, dst_ref=mask_land, send_sem=mx_ssem.at[0], recv_sem=mx_rsem.at[0],
            device_id=(my_x + 1, my_y), device_id_type=MESH,
        ))]

    def pack_copies():
        copies = []
        for index, (dx, dy) in enumerate([(0, 1), (0, -1), (1, 1), (1, -1)]):
            side = 0 if dy > 0 else 1
            copies.append((dx, dy, pltpu.make_async_remote_copy(
                src_ref=pack_send.at[side],
                dst_ref=pack_land.at[side, pl.ds((1 - dx) * rows, rows), :],
                send_sem=pk_ssem.at[index], recv_sem=pk_rsem.at[index],
                device_id=(my_x + dx, my_y + dy), device_id_type=MESH,
            )))
        return copies

    def start(copies):
        for dx, dy, copy in copies:
            pl.when(exists(dx, dy))(copy.start)

    def arrive(copies):
        for dx, dy, copy in copies:
            pl.when(exists(-dx, -dy))(copy.wait_recv)

    def leave(copies):
        for dx, dy, copy in copies:
            pl.when(exists(dx, dy))(copy.wait_send)

    def step_copies(s):
        return halo_copies(ext.at[s], edge_send.at[s], edge_land.at[s], send_sem.at[s], recv_sem.at[s])

    mat_copies = halo_copies(mat_ext, mat_send, mat_land, mat_ssem, mat_rsem)

    for read in reads[:3]:
        read.wait()
    for x in range(nx):
        at = pl.ds(rows + x * nz, nz)
        for f in range(3):
            ext[0, f, at, :] = disp_in[f, layer(x), :]
            vel[f, pl.ds(x * nz, nz), :] = vel_in[f, layer(x), :]
        labels = lab_in[layer(x), :]
        modulus = jnp.zeros(labels.shape, jnp.float32)
        limit = jnp.zeros(labels.shape, jnp.float32)
        for material in range(MATS):
            matches = labels == material
            modulus = jnp.where(matches, stiff[material], modulus)
            limit = jnp.where(matches, crit[material], limit)
        mat_ext[0, at, :] = modulus
        mat_ext[1, at, :] = limit
    own = pl.ds(rows, rows)
    pack_edges([mat_ext[f, own, :] for f in range(2)], mat_send)
    pack_edges([ext[0, f, own, :] for f in range(3)], edge_send.at[0])

    neighbours = lax.select(my_x > 0, 1, 0) + lax.select(my_x < size_x - 1, 1, 0) + 1
    neighbours = neighbours * (lax.select(my_y > 0, 1, 0) + lax.select(my_y < size_y - 1, 1, 0) + 1) - 1
    pl.semaphore_wait(barrier, neighbours)
    start(mat_copies)
    start(step_copies(0))

    reads[3].wait()

    def mask_row(k, x):
        return nz * (sum(OFFSETS[q][0] for q in range(k)) + x)

    up = jnp.zeros((rows, ny), jnp.float32)
    down = jnp.zeros((rows, ny), jnp.float32)
    for k, d in enumerate(OFFSETS):
        for x in range(nx):
            value = mask_in[k, layer(x), :].astype(jnp.float32)
            mask_ext[k, pl.ds(rows + x * nz, nz), :] = value
            if x >= nx - d[0]:
                mask_send[pl.ds(mask_row(k, x - (nx - d[0])), nz), :] = value
    start(mask_copies())
    for k, d in enumerate(OFFSETS):
        c = d[2]
        if c > 0:
            value = mask_ext[k, own, :]
            up = jnp.where(lane // 4 == SLOT[k], roll(value, c + 4 * SLOT[k]), up)
        elif c < 0:
            value = mask_ext[k, own, :]
            down = jnp.where(lane // 4 == ny // 4 - 1 - SLOT[k], roll(value, c - 4 * SLOT[k]), down)
    pack_send[0] = up
    pack_send[1] = down
    start(pack_copies())

    def shift_fields(source, land, target, count, add_step):
        full = 3 * rows
        lanes = lax.broadcasted_iota(jnp.int32, (full, ny), 1)
        for f in range(count):
            value = source[f]
            high = roll(land[1], -4 * f)
            low = roll(land[0], 4 * f)
            for c in range(-3, 4):
                moved_value = value
                if c > 0:
                    moved_value = roll(jnp.where(lanes < c, high, value), -c)
                elif c < 0:
                    moved_value = roll(jnp.where(lanes >= ny + c, low, value), -c)
                if add_step and f == 2 and c != 0:
                    moved_value = moved_value + float(c)
                target[c + 3, f] = moved_value

    arrive(mat_copies)
    shift_fields(mat_ext, mat_land, mat_moved, 2, False)

    def inside_depth(b):
        return jnp.where((depth + b >= 0) & (depth + b < nz), 1.0, 0.0).astype(jnp.float32)

    def coefficients(number, offset, live):
        a, b, c = offset
        length = math.sqrt(a * a + b * b + c * c)
        at = pl.ds(rows + nz * a + b, rows)
        here, there = mat_ext[0, own, :], mat_moved[c + 3, 0, at, :]
        limit = mat_ext[1, own, :] + mat_moved[c + 3, 1, at, :]
        square = limit * limit * (0.25 * length * length)
        if b != 0:
            live = live * inside_depth(b)
        gain[number] = (here * there) / (here + there) * (square * (2.0 / length**3)) * live
        spread[number] = square

    for number, (k, forward, offset) in enumerate(SHELL):
        if forward:
            coefficients(number, offset, mask_ext[k, own, :])

    arrive(mask_copies())
    arrive(pack_copies())
    for k in range(FLAT, len(OFFSETS)):
        a = OFFSETS[k][0]
        mask_ext[k, pl.ds(0, rows), :] = jnp.zeros((rows, ny), jnp.float32)
        mask_ext[k, pl.ds((nx - a) * nz, a * nz), :] = mask_land[pl.ds(mask_row(k, 0), a * nz), :]
    for k in range(FLAT):
        mask_ext[k, pl.ds(0, rows), :] = jnp.zeros((rows, ny), jnp.float32)
    for number, (k, forward, offset) in enumerate(SHELL):
        if not forward:
            a, b, c = OFFSETS[k]
            at = pl.ds(rows - nz * a - b, rows)
            live = roll(mask_ext[k, at, :], c)
            if c > 0:
                live = jnp.where(lane < c, roll(pack_land[0, at, :], -4 * SLOT[k]), live)
            elif c < 0:
                live = jnp.where(lane >= ny + c, roll(pack_land[1, at, :], 4 * SLOT[k]), live)
            coefficients(number, offset, live)

    def one_step(s, carry):
        arrive(step_copies(s))
        shift_fields(ext.at[s], edge_land.at[s], moved, 3, True)
        here = [ext[s, f, own, :] for f in range(3)]
        force = [jnp.zeros((rows, ny), jnp.float32) for _ in range(3)]
        for number, (k, forward, offset) in enumerate(SHELL):
            a, b, c = offset
            length = math.sqrt(a * a + b * b + c * c)
            at = pl.ds(rows + nz * a + b, rows)
            e = [
                moved[c + 3, 0, at, :] - (here[0] - float(a)),
                moved[c + 3, 1, at, :] - (here[1] - float(b)),
                moved[c + 3, 2, at, :] - here[2],
            ]
            square = jnp.maximum(e[0] * e[0] + e[1] * e[1] + e[2] * e[2], 1e-30)
            t = square * lax.rsqrt(square) - length
            magnitude = gain[number] * t / (spread[number] + t * t)
            force = [force[f] + magnitude * e[f] for f in range(3)]
        fresh = []
        for f in range(3):
            velocity = vel[f] + time_step * force[f]
            vel[f] = velocity
            fresh.append(here[f] + time_step * velocity)

        @pl.when(s < STEPS - 1)
        def _():
            for f in range(3):
                ext[s + 1, f, own, :] = fresh[f]
            pack_edges(fresh, edge_send.at[s + 1])
            start(step_copies(s + 1))

        @pl.when(s == STEPS - 1)
        def _():
            for f in range(3):
                moved[3, f, pl.ds(0, rows), :] = fresh[f]
        return carry

    lax.fori_loop(0, STEPS, one_step, 0)
    for f in range(3):
        for x in range(nx):
            disp_out[f, layer(x), :] = moved[3, f, pl.ds(x * nz, nz), :]
            vel_out[f, layer(x), :] = vel[f, pl.ds(x * nz, nz), :]

    leave(mat_copies)
    leave(mask_copies())
    leave(pack_copies())

    def drain(s, carry):
        leave(step_copies(s))
        return carry

    lax.fori_loop(0, STEPS, drain, 0)


def on_device(displacement, velocity, labels, bond_mask, stiffness, critical):
    nx, nz, ny = labels.shape
    rows = nx * nz
    count = len(SHELL)
    edge_rows = -(-nz * sum(d[0] for d in OFFSETS) // 8) * 8

    def by_depth(value):
        lead = value.shape[:-3]
        order = tuple(range(len(lead))) + tuple(len(lead) + i for i in (1, 0, 2))
        return value.transpose(order).reshape(lead + (rows, ny))

    f32 = jnp.float32
    vmem, smem = pl.BlockSpec(memory_space=pltpu.VMEM), pl.BlockSpec(memory_space=pltpu.SMEM)
    dma = pltpu.SemaphoreType.DMA
    results = pl.pallas_call(
        functools.partial(kernel, (nx, nz, ny)),
        out_shape=[jax.ShapeDtypeStruct((3, rows, ny), f32)] * 2,
        in_specs=[pl.BlockSpec(memory_space=pltpu.HBM)] * 4 + [smem] * 2,
        out_specs=[vmem] * 2,
        scratch_shapes=[
            pltpu.VMEM((3, rows, ny), f32),
            pltpu.VMEM((3, rows, ny), f32),
            pltpu.VMEM((rows, ny), jnp.int32),
            pltpu.VMEM((len(OFFSETS), rows, ny), jnp.int32),
            dma((4,)),
            pltpu.VMEM((STEPS, 3, 3 * rows, ny), f32),
            pltpu.VMEM((STEPS, 2, rows, ny), f32),
            pltpu.VMEM((STEPS, 2, 3 * rows, ny), f32),
            pltpu.VMEM((2, 3 * rows, ny), f32),
            pltpu.VMEM((2, rows, ny), f32),
            pltpu.VMEM((2, 3 * rows, ny), f32),
            pltpu.VMEM((edge_rows, ny), f32),
            pltpu.VMEM((edge_rows, ny), f32),
            pltpu.VMEM((len(OFFSETS), 2 * rows, ny), f32),
            pltpu.VMEM((2, rows, ny), f32),
            pltpu.VMEM((2, 2 * rows, ny), f32),
            pltpu.VMEM((7, 3, 3 * rows, ny), f32),
            pltpu.VMEM((7, 2, 3 * rows, ny), f32),
            pltpu.VMEM((count, rows, ny), f32),
            pltpu.VMEM((count, rows, ny), f32),
            pltpu.VMEM((3, rows, ny), f32),
            dma((STEPS, 8)), dma((STEPS, 8)), dma((8,)), dma((8,)),
            dma((1,)), dma((1,)), dma((4,)), dma((4,)),
        ],
        compiler_params=pltpu.CompilerParams(
            collective_id=0, has_side_effects=True, vmem_limit_bytes=63 * 1024 * 1024 + 960 * 1024
        ),
        name="peridynamics",
    )(
        by_depth(displacement), by_depth(velocity), by_depth(labels), by_depth(bond_mask),
        stiffness, critical,
    )
    return tuple(value.reshape(3, nz, nx, ny).transpose(0, 2, 1, 3) for value in results)


def solution(mesh):
    in_specs = (
        P(None, "wx", None, "ny"),
        P(None, "wx", None, "ny"),
        P("wx", None, "ny"),
        P(None, "wx", None, "ny"),
        P(),
        P(),
    )
    out_specs = (P(None, "wx", None, "ny"), P(None, "wx", None, "ny"))
    return jax.shard_map(
        on_device, mesh=mesh, in_specs=in_specs, out_specs=out_specs, check_vma=False
    )
```
